32 devices in a mesh: rows: 8 (over y, x, core), feat: 4 (over z).
Axes of the slice: x: 2, y: 2, z: 4, core: 2. Of those that a mesh axis runs over, the one named last changes fastest.
Arguments:
- node_feats: bfloat16 [256, 32768], P('feat', 'rows'), may hold values from -6 to 6
- tile_vals: bfloat16 [256, 16, 128, 128], P('rows'), may hold values from -0.125 to 0.125
- tile_cols: int32 [256, 16], P('rows'), may hold values from 0 to 255, as said below
- weight: bfloat16 [256, 256], P(None, 'feat'), may hold values from -0.375 to 0.375
- bias_vec: float32 [256], P('feat'), may hold values from -3 to 3
- grad_out: bfloat16 [256, 32768], P('feat', 'rows'), may hold values from -6 to 6
Outputs:
- activated: bfloat16 [256, 32768], P('feat', 'rows')
- grad_feats: float32 [256, 32768], P('feat', 'rows')
- grad_weight: float32 [256, 256], P(None, 'feat')
- grad_bias: float32 [256], P('feat')
The draws below stay inside these ranges and needn't reach their ends.
Inputs may be any that keep to these rules, and one draw needn't show every extreme that they name: `tile_cols`: among the tiles of one device's 32 blocks of rows, the column blocks held by any one owner (blocks o * 32 to o * 32 + 31) are at most 16 distinct ones and at least one; on every device some owner reaches 16.
All inputs are finite; a program needn't handle non-finite values.
Results may differ from the reference program's by a relative error of at most 0.007.
Values may be sent and summed in bfloat16 or wider, within the bound.
A program may use at most 256 MiB of HBM per device.

```python
import jax
import jax.numpy as jnp
from jax import lax

FEAT = 256
TB = 128
SLOTS = 16
BLK_DEV = 32
CAP = 16
NODE_BLOCKS = 256
NODES = 32768
N_ROWS = 8


def draw_tile_cols(key, part):
    keys = jax.random.split(key, 6)
    row_devs = NODE_BLOCKS // BLK_DEV
    tiles = BLK_DEV * SLOTS
    listed = row_devs * CAP
    counts = jax.random.randint(keys[0], (row_devs, row_devs), 1, CAP + 1)
    full_owner = jax.random.randint(keys[1], (row_devs,), 0, row_devs)
    counts = jnp.where(jnp.arange(row_devs)[None, :] == full_owner[:, None], CAP, counts)
    scores = jax.random.randint(keys[2], (row_devs, row_devs, BLK_DEV), 0, 1 << 20) * BLK_DEV + jnp.arange(BLK_DEV)
    orders = jnp.argsort(scores, axis=-1)
    entries = jnp.arange(listed)
    entry_owner = entries // CAP
    entry_rank = entries % CAP
    valid = entry_rank[None, :] < counts[:, entry_owner]
    spare_owner = jax.random.randint(keys[3], (row_devs, tiles), 0, row_devs)
    spare_draw = jax.random.randint(keys[4], (row_devs, tiles), 0, 1 << 20)
    spare_rank = spare_draw % jnp.take_along_axis(counts, spare_owner, axis=1)
    places = jnp.arange(tiles)
    clipped = jnp.minimum(places, listed - 1)
    use_list = (places < listed)[None, :] & jnp.take(valid, clipped, axis=1)
    owners = jnp.where(use_list, entry_owner[clipped][None, :], spare_owner)
    ranks = jnp.where(use_list, entry_rank[clipped][None, :], spare_rank)
    chosen = orders[jnp.arange(row_devs)[:, None], owners, ranks]
    columns = owners * BLK_DEV + chosen
    shuffle = jax.random.randint(keys[5], (row_devs, tiles), 0, 1 << 20) * tiles + places
    columns = jnp.take_along_axis(columns, jnp.argsort(shuffle, axis=-1), axis=1)
    return columns.reshape(NODE_BLOCKS, SLOTS).astype(jnp.int32)


def level_of(rng, shape, cuts, least, largest):
    gain, own = 1.0, jax.random.fold_in(rng, 6)
    for axis_at, parts in cuts:
        heights = jnp.exp(jax.random.uniform(jax.random.fold_in(own, axis_at), (parts,), jnp.float32, least / len(cuts), largest / len(cuts)))
        gain = gain * jnp.repeat(heights, shape[axis_at] // parts).reshape([-1 if axis == axis_at else 1 for axis in range(len(shape))])
    return gain


def scatter_about(own_key, extent, scale, reach, cuts=(), dtype=jnp.bfloat16):
    loudness = level_of(own_key, extent, cuts, -0.22, 0.18) if cuts else 1.0
    values = jax.random.normal(own_key, extent, jnp.float32) * scale * loudness
    return jnp.minimum(jnp.maximum(values, -reach), reach).astype(dtype)


def setup_inputs(seed: int = 0) -> dict:
    key_list = jax.random.split(jax.random.key(seed), 7)
    return {
        "node_feats": scatter_about(key_list[0], (FEAT, NODES), 1.0, 6.0, ((0, 4), (1, 8))),
        "tile_vals": scatter_about(key_list[1], (NODE_BLOCKS, SLOTS, TB, TB), (SLOTS * TB) ** -0.5, 0.125, ((0, 8),)),
        "tile_cols": draw_tile_cols(jax.random.fold_in(key_list[6], 71), 0),
        "weight": scatter_about(key_list[3], (FEAT, FEAT), FEAT ** -0.5, 0.375, ((1, 4),)),
        "bias_vec": scatter_about(key_list[4], (FEAT,), 0.5, 3.0, ((0, 4),), jnp.float32),
        "grad_out": scatter_about(key_list[5], (FEAT, NODES), 1.0, 6.0, ((0, 4), (1, 8))),
    }


def aggregate(node_feats, tile_vals, tile_cols):
    blocks = node_feats.reshape(FEAT, NODE_BLOCKS, TB)

    def one_device(inputs):
        values, columns = inputs
        chosen = jnp.take(blocks, columns.reshape(-1).astype(jnp.int32), axis=1)
        chosen = chosen.reshape(FEAT, BLK_DEV, SLOTS, TB)
        return jnp.einsum('fisb,isab->fia', chosen.astype(jnp.float32), values.astype(jnp.float32))

    result = lax.map(one_device, (tile_vals.reshape(N_ROWS, BLK_DEV, SLOTS, TB, TB), tile_cols.reshape(N_ROWS, BLK_DEV, SLOTS)))
    return result.transpose(1, 0, 2, 3).reshape(FEAT, NODES)


def spread(back_mix, tile_vals, tile_cols):
    pieces = back_mix.reshape(FEAT, N_ROWS, BLK_DEV, TB).transpose(1, 0, 2, 3)

    def advance(running, inputs):
        mixed, values, columns = inputs
        contrib = jnp.einsum('fia,isab->fisb', mixed.astype(jnp.float32), values.astype(jnp.float32))
        running = running.at[:, columns.reshape(-1).astype(jnp.int32)].add(contrib.reshape(FEAT, BLK_DEV * SLOTS, TB))
        return running, None

    running, _ = lax.scan(advance, jnp.zeros((FEAT, NODE_BLOCKS, TB), jnp.float32), (pieces, tile_vals.reshape(N_ROWS, BLK_DEV, SLOTS, TB, TB), tile_cols.reshape(N_ROWS, BLK_DEV, SLOTS)))
    return running.reshape(FEAT, NODES)


def reference(node_feats, tile_vals, tile_cols, weight, bias_vec, grad_out):
    aggregated = aggregate(node_feats, tile_vals, tile_cols).astype(jnp.bfloat16)
    preact = jnp.dot(weight.T, aggregated, preferred_element_type=jnp.float32) + bias_vec[:, None]
    sigma = jax.nn.sigmoid(preact)
    activated = (preact * sigma).astype(jnp.bfloat16)
    grad_pre = (grad_out.astype(jnp.float32) * sigma * (1.0 + preact * (1.0 - sigma))).astype(jnp.bfloat16)
    grad_weight = jnp.dot(aggregated, grad_pre.T, preferred_element_type=jnp.float32)
    grad_bias = jnp.sum(grad_pre.astype(jnp.float32), axis=1)
    back_mix = jnp.dot(weight, grad_pre, preferred_element_type=jnp.float32).astype(jnp.bfloat16)
    grad_feats = spread(back_mix, tile_vals, tile_cols)
    return activated, grad_feats, grad_weight, grad_bias
```

```python
import functools

import jax
import jax.numpy as jnp
from jax import lax
from jax.experimental import pallas as pl
from jax.experimental.pallas import tpu as pltpu
from jax.sharding import PartitionSpec as P

MESH = pl.DeviceIdType.MESH
BF16 = jnp.bfloat16
F32 = jnp.float32
VMEM_BYTES = 60 * 1024 * 1024


def flip(index, mask, count):
    out, place = 0, 1
    while place < count:
        bit = (index // place) % 2
        out = out + ((1 - bit) if mask & place else bit) * place
        place *= 2
    return out


def greet(rows_peers, feat_peers):
    barrier = pltpu.get_barrier_semaphore()
    for peer in rows_peers:
        pl.semaphore_signal(barrier, inc=1, device_id={"rows": peer}, device_id_type=MESH)
    for peer in feat_peers:
        pl.semaphore_signal(barrier, inc=1, device_id={"feat": peer}, device_id_type=MESH)
    pl.semaphore_wait(barrier, len(rows_peers) + len(feat_peers))


def remote(src, dst, send_sem, recv_sem, **where):
    return pltpu.make_async_remote_copy(
        src_ref=src, dst_ref=dst, send_sem=send_sem, recv_sem=recv_sem,
        device_id=where, device_id_type=MESH,
    )


def forward_kernel(
    n_rows, n_feat,
    cols_ref, x_ref, gout_ref, wt_ref, bias_ref, tiles_hbm,
    bm_in, act_out, gw_ref, gb_ref,
    xall, gsend, gall, wall, ball, tiles, agg_send, agg_in, bm_send,
    tile_sem, x_send, x_recv, f_send, f_recv, g_send, g_recv, w_send, w_recv,
    b_send, b_recv, a_send, a_recv, m_send, m_recv,
):
    me_r, me_f = lax.axis_index("rows"), lax.axis_index("feat")
    feat_loc = x_ref.shape[0]
    blocks, slots, edge = tiles_hbm.shape[0], tiles_hbm.shape[1], tiles_hbm.shape[2]
    quarter = blocks // n_feat
    n_chip = n_rows // 2
    chip, core = me_r // 2, me_r % 2
    mate = me_r + 1 - 2 * core
    chips = [flip(chip, p, n_chip) for p in range(n_chip)]
    peers_f = [(me_f + j) % n_feat for j in range(n_feat)]
    from_f = [(me_f + n_feat - j) % n_feat for j in range(n_feat)]

    def owned(row):
        return xall.at[pl.ds(row * blocks, blocks)]

    @pl.loop(0, blocks)
    def _(i):
        pltpu.make_async_copy(tiles_hbm.at[i], tiles.at[i], tile_sem.at[i]).start()

    for i in range(blocks):
        xall[me_r * blocks + i] = x_ref[:, i * edge:(i + 1) * edge]
        gsend[i // quarter, i % quarter] = gout_ref[:, i * edge:(i + 1) * edge]

    greet([mate] + [chips[p] * 2 + core for p in range(1, n_chip)], peers_f[1:])

    x_out = []
    for p in range(1, n_chip):
        x_out.append(remote(owned(me_r), owned(me_r), x_send.at[p], x_recv.at[p], rows=chips[p] * 2 + core))
    x_out.append(remote(owned(me_r), owned(me_r), x_send.at[0], x_recv.at[0], rows=mate))
    for copy in x_out:
        copy.start()
    z_out = []
    for j in range(1, n_feat):
        z_out.append(remote(gsend.at[peers_f[j]], gall.at[me_f], g_send.at[j], g_recv.at[j], feat=peers_f[j]))
        z_out.append(remote(wt_ref, wall.at[me_f], w_send.at[j], w_recv.at[j], feat=peers_f[j]))
        z_out.append(remote(bias_ref, ball.at[me_f], b_send.at[j], b_recv.at[j], feat=peers_f[j]))
    for copy in z_out:
        copy.start()
    gall[me_f] = gsend[me_f]
    wall[me_f] = wt_ref[...]
    ball[me_f] = bias_ref[...]

    for p in range(1, n_chip):
        src = chips[p] * 2 + core
        remote(owned(src), owned(src), x_send.at[p], x_recv.at[p], rows=mate).wait_recv()
        passed = remote(owned(src), owned(src), f_send.at[p], f_recv.at[p], rows=mate)
        passed.start()
        x_out.append(passed)
    remote(owned(mate), owned(mate), x_send.at[0], x_recv.at[0], rows=mate).wait_recv()
    for p in range(1, n_chip):
        src = chips[p] * 2 + 1 - core
        remote(owned(src), owned(src), f_send.at[p], f_recv.at[p], rows=mate).wait_recv()

    agg_out = []
    for j in range(1, n_feat + 1):
        q = peers_f[j % n_feat]

        @pl.loop(0, quarter)
        def _(k):
            i = q * quarter + k
            pltpu.make_async_copy(tiles_hbm.at[i], tiles.at[i], tile_sem.at[i]).wait()
            picked = jnp.concatenate([xall[cols_ref[i, s]] for s in range(slots)], axis=1)
            vals = jnp.concatenate([tiles[i, s] for s in range(slots)], axis=1)
            agg = lax.dot_general(picked, vals, (((1,), (1,)), ((), ())), preferred_element_type=F32)
            agg_send[q, k] = agg.astype(BF16)

        if j < n_feat:
            copy = remote(agg_send.at[q], agg_in.at[me_f], a_send.at[j], a_recv.at[j], feat=q)
            copy.start()
            agg_out.append(copy)
    agg_in[me_f] = agg_send[me_f]

    for copy in z_out:
        copy.wait()
    for copy in agg_out:
        copy.wait()

    feat = n_feat * feat_loc
    gw_ref[...] = jnp.zeros_like(gw_ref)
    gb_ref[...] = jnp.zeros_like(gb_ref)
    pair = 2 if quarter % 2 == 0 else 1

    @pl.loop(0, quarter // pair)
    def _(t):
        def joined(ref):
            return jnp.concatenate([ref[:, t * pair + u].reshape(feat, edge) for u in range(pair)], axis=1)

        wt = wall[...].reshape(feat, feat)
        agg = joined(agg_in)
        preact = jnp.dot(wt, agg, preferred_element_type=F32)
        preact = preact + jnp.concatenate([ball[...].reshape(feat, edge)] * pair, axis=1)
        sigma = jax.nn.sigmoid(preact)
        act = (preact * sigma).astype(BF16)
        grad = (joined(gall).astype(F32) * sigma * (1.0 + preact * (1.0 - sigma))).astype(BF16)
        mix = lax.dot_general(wt, grad, (((0,), (0,)), ((), ())), preferred_element_type=F32).astype(BF16)
        gw_ref[...] += lax.dot_general(agg, grad, (((1,), (1,)), ((), ())), preferred_element_type=F32)
        grad32 = grad.astype(F32)
        for u in range(pair):
            cut = slice(u * edge, (u + 1) * edge)
            act_out[:, t * pair + u] = act[:, cut].reshape(n_feat, feat_loc, edge)
            bm_send[:, t * pair + u] = mix[:, cut].reshape(n_feat, feat_loc, edge)
            gb_ref[...] += grad32[:, cut]

    m_out = []
    for j in range(1, n_feat):
        copy = remote(bm_send.at[peers_f[j]], bm_in.at[me_f], m_send.at[j], m_recv.at[j], feat=peers_f[j])
        copy.start()
        m_out.append(copy)
    bm_in[me_f] = bm_send[me_f]
    for copy in x_out:
        copy.wait_send()
    for copy in m_out:
        copy.wait()


def spread_kernel(blocks, slots, edge, cols_ref, bm_ref, tiles_ref, terms_ref, acc):
    step = pl.program_id(0)

    @pl.when(step == 0)
    def _():
        acc[...] = jnp.zeros_like(acc)

    @pl.when(step < blocks)
    def _():
        vals = jnp.concatenate([tiles_ref[0, s] for s in range(slots)], axis=1)
        contrib = jnp.dot(bm_ref[step], vals, preferred_element_type=F32)
        for s in range(slots):
            col = cols_ref[step, s]
            acc[col] = acc[col] + contrib[:, s * edge:(s + 1) * edge]

    @pl.when(step >= blocks)
    def _():
        first = (step - blocks) * blocks
        terms_ref[...] = acc[pl.ds(first, blocks)].astype(BF16)


def collect_kernel(
    n_rows, n_feat, terms_ref, act_ref, gf_ref, out_ref,
    mate_in, sums, chip_in, act_in,
    t_send, t_recv, c_send, c_recv, a_send, a_recv,
):
    me_r, me_f = lax.axis_index("rows"), lax.axis_index("feat")
    blocks = terms_ref.shape[0] // n_rows
    edge = terms_ref.shape[2]
    quarter = blocks // n_feat
    n_chip = n_rows // 2
    chip, core = me_r // 2, me_r % 2
    mate = me_r + 1 - 2 * core
    chips = [flip(chip, p, n_chip) for p in range(n_chip)]
    peers_f = [(me_f + j) % n_feat for j in range(n_feat)]
    greet([mate] + [chips[p] * 2 + core for p in range(1, n_chip)], peers_f[1:])

    order = list(range(1, n_chip)) + [0]
    to_mate = {}
    for p in order:
        owner = chips[p] * 2 + 1 - core
        to_mate[p] = remote(terms_ref.at[pl.ds(owner * blocks, blocks)], mate_in.at[p],
                            t_send.at[p], t_recv.at[p], rows=mate)
        to_mate[p].start()
    act_out = []
    for j in range(1, n_feat):
        copy = remote(act_ref.at[peers_f[j]], act_in.at[me_f], a_send.at[j], a_recv.at[j], feat=peers_f[j])
        copy.start()
        act_out.append(copy)
    act_in[me_f] = act_ref[me_f]
    to_chip = {}
    for p in order:
        to_mate[p].wait_recv()
        if p:
            owner = chips[p] * 2 + core

            @pl.loop(0, blocks)
            def _(i):
                sums[p, i] = (terms_ref[owner * blocks + i].astype(F32) + mate_in[p, i].astype(F32)).astype(BF16)

            to_chip[p] = remote(sums.at[p], chip_in.at[p], c_send.at[p], c_recv.at[p], rows=owner)
            to_chip[p].start()
    for copy in act_out:
        copy.wait()
    for i in range(blocks):
        out_ref[:, i * edge:(i + 1) * edge] = act_in[i // quarter, i % quarter]
    for p in range(1, n_chip):
        to_chip[p].wait_recv()
    for i in range(blocks):
        total = terms_ref[me_r * blocks + i].astype(F32) + mate_in[0, i].astype(F32)
        for p in range(1, n_chip):
            total = total + chip_in[p, i].astype(F32)
        gf_ref[:, i * edge:(i + 1) * edge] = total
    for p in order:
        to_mate[p].wait_send()
        if p:
            to_chip[p].wait_send()


def on_device(node_feats, tile_vals, tile_cols, weight, bias_vec, grad_out):
    n_rows, n_feat = lax.axis_size("rows"), lax.axis_size("feat")
    feat_loc = node_feats.shape[0]
    blocks, slots, edge = tile_vals.shape[0], tile_vals.shape[1], tile_vals.shape[2]
    feat = feat_loc * n_feat
    quarter = blocks // n_feat
    n_chip = n_rows // 2
    vmem = pl.BlockSpec(memory_space=pltpu.VMEM)
    dma = pltpu.SemaphoreType.DMA
    flops = 2 * feat_loc * blocks * slots * edge * edge
    tile_bytes = 2 * blocks * slots * edge * edge

    parts = (n_feat, quarter, feat_loc, edge)
    bm, act, gw, gb = pl.pallas_call(
        functools.partial(forward_kernel, n_rows, n_feat),
        out_shape=(
            jax.ShapeDtypeStruct(parts, BF16),
            jax.ShapeDtypeStruct(parts, BF16),
            jax.ShapeDtypeStruct((feat, feat), F32),
            jax.ShapeDtypeStruct((feat, edge), F32),
        ),
        in_specs=[pl.BlockSpec(memory_space=pltpu.SMEM), vmem, vmem, vmem, vmem,
                  pl.BlockSpec(memory_space=pl.ANY)],
        out_specs=(vmem,) * 4,
        scratch_shapes=[
            pltpu.VMEM((n_rows * blocks, feat_loc, edge), BF16),
            pltpu.VMEM(parts, BF16),
            pltpu.VMEM(parts, BF16),
            pltpu.VMEM((n_feat, feat_loc, feat), BF16),
            pltpu.VMEM((n_feat, feat_loc, edge), F32),
            pltpu.VMEM((blocks, slots, edge, edge), BF16),
            pltpu.VMEM(parts, BF16),
            pltpu.VMEM(parts, BF16),
            pltpu.VMEM(parts, BF16),
            dma((blocks,)),
        ] + [dma((n_chip,))] * 4 + [dma((n_feat,))] * 10,
        compiler_params=pltpu.CompilerParams(
            collective_id=0, has_side_effects=True, vmem_limit_bytes=VMEM_BYTES),
        cost_estimate=pl.CostEstimate(flops=flops, bytes_accessed=tile_bytes, transcendentals=0),
        name="aggregate_and_mix",
    )(tile_cols, node_feats, grad_out, weight.T,
      jnp.broadcast_to(bias_vec[:, None], (feat_loc, edge)), tile_vals)

    gb = jnp.sum(gb, axis=1)
    grad_weight = lax.psum_scatter(gw, "feat", scatter_dimension=1, tiled=True)
    grad_bias = lax.psum_scatter(gb, "feat", scatter_dimension=0, tiled=True)
    grad_weight, grad_bias = lax.psum((grad_weight, grad_bias), "rows")

    terms = pl.pallas_call(
        functools.partial(spread_kernel, blocks, slots, edge),
        out_shape=jax.ShapeDtypeStruct((n_rows * blocks, feat_loc, edge), BF16),
        grid_spec=pltpu.PrefetchScalarGridSpec(
            num_scalar_prefetch=1,
            grid=(blocks + n_rows,),
            in_specs=[
                pl.BlockSpec((blocks, feat_loc, edge), lambda i, cols: (0, 0, 0)),
                pl.BlockSpec((1, slots, edge, edge), lambda i, cols: (jnp.minimum(i, blocks - 1), 0, 0, 0)),
            ],
            out_specs=pl.BlockSpec((blocks, feat_loc, edge), lambda i, cols: (jnp.maximum(i - blocks, 0), 0, 0)),
            scratch_shapes=[pltpu.VMEM((n_rows * blocks, feat_loc, edge), F32)],
        ),
        compiler_params=pltpu.CompilerParams(vmem_limit_bytes=VMEM_BYTES),
        cost_estimate=pl.CostEstimate(flops=flops, bytes_accessed=tile_bytes, transcendentals=0),
        name="spread_terms",
    )(tile_cols, bm.reshape(blocks, feat_loc, edge), tile_vals)

    grad_feats, activated = pl.pallas_call(
        functools.partial(collect_kernel, n_rows, n_feat),
        out_shape=(
            jax.ShapeDtypeStruct((feat_loc, blocks * edge), F32),
            jax.ShapeDtypeStruct((feat_loc, blocks * edge), BF16),
        ),
        in_specs=[vmem, vmem],
        out_specs=(vmem, vmem),
        scratch_shapes=[pltpu.VMEM((n_chip, blocks, feat_loc, edge), BF16)] * 3
        + [pltpu.VMEM(parts, BF16)]
        + [dma((n_chip,))] * 4 + [dma((n_feat,))] * 2,
        compiler_params=pltpu.CompilerParams(
            collective_id=1, has_side_effects=True, vmem_limit_bytes=VMEM_BYTES),
        cost_estimate=pl.CostEstimate(flops=1, bytes_accessed=tile_bytes // 4, transcendentals=0),
        name="collect_terms",
    )(terms, act)
    return activated, grad_feats, grad_weight, grad_bias


def solution(mesh):
    placed = (
        P("feat", "rows"),
        P("rows", None, None, None),
        P("rows", None),
        P(None, "feat"),
        P("feat"),
        P("feat", "rows"),
    )
    return jax.shard_map(
        on_device,
        mesh=mesh,
        in_specs=placed,
        out_specs=(P("feat", "rows"), P("feat", "rows"), P(None, "feat"), P("feat")),
        check_vma=False,
    )
```

```python
import functools

import jax
import jax.numpy as jnp
from jax import lax
from jax.experimental import pallas as pl
from jax.experimental.pallas import tpu as pltpu
from jax.sharding import PartitionSpec as P

MESH = pl.DeviceIdType.MESH
BF16 = jnp.bfloat16
F32 = jnp.float32
VMEM_BYTES = 60 * 1024 * 1024


def flip(index, mask, count):
    out, place = 0, 1
    while place < count:
        bit = (index // place) % 2
        out = out + ((1 - bit) if mask & place else bit) * place
        place *= 2
    return out


def greet(rows_peers, feat_peers):
    barrier = pltpu.get_barrier_semaphore()
    for peer in rows_peers:
        pl.semaphore_signal(barrier, inc=1, device_id={"rows": peer}, device_id_type=MESH)
    for peer in feat_peers:
        pl.semaphore_signal(barrier, inc=1, device_id={"feat": peer}, device_id_type=MESH)
    pl.semaphore_wait(barrier, len(rows_peers) + len(feat_peers))


def remote(src, dst, send_sem, recv_sem, **where):
    return pltpu.make_async_remote_copy(
        src_ref=src, dst_ref=dst, send_sem=send_sem, recv_sem=recv_sem,
        device_id=where, device_id_type=MESH,
    )


def forward_kernel(
    n_rows, n_feat,
    cols_ref, x_ref, gout_ref, wt_ref, bias_ref, tiles_hbm,
    bm_in, act_out, gw_ref,
    xall, gsend, gall, wall, ball, tiles, agg_send, agg_in, bm_send,
    tile_sem, x_send, x_recv, f_send, f_recv, g_send, g_recv, w_send, w_recv,
    b_send, b_recv, a_send, a_recv, m_send, m_recv,
):
    me_r, me_f = lax.axis_index("rows"), lax.axis_index("feat")
    feat_loc = x_ref.shape[0]
    blocks, slots, edge = tiles_hbm.shape[0], tiles_hbm.shape[1], tiles_hbm.shape[2]
    quarter = blocks // n_feat
    n_chip = n_rows // 2
    chip, core = me_r // 2, me_r % 2
    mate = me_r + 1 - 2 * core
    chips = [flip(chip, p, n_chip) for p in range(n_chip)]
    peers_f = [(me_f + j) % n_feat for j in range(n_feat)]
    from_f = [(me_f + n_feat - j) % n_feat for j in range(n_feat)]

    def owned(row):
        return xall.at[pl.ds(row * blocks, blocks)]

    @pl.loop(0, blocks)
    def _(i):
        pltpu.make_async_copy(tiles_hbm.at[i], tiles.at[i], tile_sem.at[i]).start()

    for i in range(blocks):
        xall[me_r * blocks + i] = x_ref[:, i * edge:(i + 1) * edge]
        gsend[i // quarter, i % quarter] = gout_ref[:, i * edge:(i + 1) * edge]

    greet([mate] + [chips[p] * 2 + core for p in range(1, n_chip)], peers_f[1:])

    x_out = []
    for p in range(1, n_chip):
        x_out.append(remote(owned(me_r), owned(me_r), x_send.at[p], x_recv.at[p], rows=chips[p] * 2 + core))
    x_out.append(remote(owned(me_r), owned(me_r), x_send.at[0], x_recv.at[0], rows=mate))
    for copy in x_out:
        copy.start()
    z_out = []
    for j in range(1, n_feat):
        z_out.append(remote(gsend.at[peers_f[j]], gall.at[me_f], g_send.at[j], g_recv.at[j], feat=peers_f[j]))
        z_out.append(remote(wt_ref, wall.at[me_f], w_send.at[j], w_recv.at[j], feat=peers_f[j]))
        z_out.append(remote(bias_ref, ball.at[me_f], b_send.at[j], b_recv.at[j], feat=peers_f[j]))
    for copy in z_out:
        copy.start()
    gall[me_f] = gsend[me_f]
    wall[me_f] = wt_ref[...]
    ball[me_f] = bias_ref[...]

    for p in range(1, n_chip):
        src = chips[p] * 2 + core
        remote(owned(src), owned(src), x_send.at[p], x_recv.at[p], rows=mate).wait_recv()
        passed = remote(owned(src), owned(src), f_send.at[p], f_recv.at[p], rows=mate)
        passed.start()
        x_out.append(passed)
    remote(owned(mate), owned(mate), x_send.at[0], x_recv.at[0], rows=mate).wait_recv()
    for p in range(1, n_chip):
        src = chips[p] * 2 + 1 - core
        remote(owned(src), owned(src), f_send.at[p], f_recv.at[p], rows=mate).wait_recv()

    group = 4 if quarter % 4 == 0 else 1
    agg_out = []
    for j in range(1, n_feat + 1):
        q = peers_f[j % n_feat]

        @pl.loop(0, quarter // group)
        def _(g):
            first = q * quarter + g * group
            for u in range(group):
                pltpu.make_async_copy(tiles_hbm.at[first + u], tiles.at[first + u], tile_sem.at[first + u]).wait()
            for u in range(group):
                i = first + u
                picked = jnp.concatenate([xall[cols_ref[s, i]] for s in range(slots)], axis=1)
                vals = jnp.concatenate([tiles[i, s] for s in range(slots)], axis=1)
                agg = lax.dot_general(picked, vals, (((1,), (1,)), ((), ())), preferred_element_type=F32)
                agg_send[q, g * group + u] = agg.astype(BF16)

        if j < n_feat:
            copy = remote(agg_send.at[q], agg_in.at[me_f], a_send.at[j], a_recv.at[j], feat=q)
            copy.start()
            agg_out.append(copy)
    agg_in[me_f] = agg_send[me_f]

    for copy in z_out:
        copy.wait()
    for copy in agg_out:
        copy.wait()

    feat = n_feat * feat_loc
    gw_ref[...] = jnp.zeros_like(gw_ref)
    pair = 2 if quarter % 2 == 0 else 1

    def mix_copy(j, t):
        part = pl.ds(t * pair, pair)
        return remote(bm_send.at[peers_f[j], part], bm_in.at[me_f, part],
                      m_send.at[j, t], m_recv.at[j, t], feat=peers_f[j])

    @pl.loop(0, quarter // pair)
    def _(t):
        def joined(ref):
            return jnp.concatenate([ref[:, t * pair + u].reshape(feat, edge) for u in range(pair)], axis=1)

        wt = wall[...].reshape(feat, feat)
        agg = joined(agg_in)
        preact = jnp.dot(wt, agg, preferred_element_type=F32)
        preact = preact + jnp.concatenate([ball[...].reshape(feat, edge)] * pair, axis=1)
        sigma = jax.nn.sigmoid(preact)
        act = (preact * sigma).astype(BF16)
        grad = (joined(gall).astype(F32) * sigma * (1.0 + preact * (1.0 - sigma))).astype(BF16)
        mix = lax.dot_general(wt, grad, (((0,), (0,)), ((), ())), preferred_element_type=F32).astype(BF16)
        part = lax.dot_general(grad, agg, (((1,), (1,)), ((), ())), preferred_element_type=F32)
        gw_ref[:, :, :feat] += part.reshape(n_feat, feat_loc, feat)
        grad32 = grad.astype(F32)
        for u in range(pair):
            cut = slice(u * edge, (u + 1) * edge)
            act_out[:, t * pair + u] = act[:, cut].reshape(n_feat, feat_loc, edge)
            bm_send[:, t * pair + u] = mix[:, cut].reshape(n_feat, feat_loc, edge)
            gw_ref[:, :, feat:] += grad32[:, cut].reshape(n_feat, feat_loc, edge)
        for j in range(1, n_feat):
            mix_copy(j, t).start()

    bm_in[me_f] = bm_send[me_f]
    for copy in x_out:
        copy.wait_send()
    @pl.loop(0, quarter // pair)
    def _(t):
        for j in range(1, n_feat):
            mix_copy(j, t).wait()


def spread_kernel(blocks, slots, edge, group, cols_ref, bm_ref, tiles_ref, terms_ref, acc):
    step = pl.program_id(0)
    steps = blocks // group

    @pl.when(step == 0)
    def _():
        acc[...] = jnp.zeros_like(acc)

    @pl.when(step < steps)
    def _():
        for u in range(group):
            i = step * group + u
            vals = jnp.concatenate([tiles_ref[u, s] for s in range(slots)], axis=1)
            contrib = jnp.dot(bm_ref[i], vals, preferred_element_type=F32)
            for s in range(slots):
                col = cols_ref[s, i]
                acc[col] = acc[col] + contrib[:, s * edge:(s + 1) * edge]

    @pl.when(step >= steps)
    def _():
        count = terms_ref.shape[0]
        first = (step - steps) * count
        terms_ref[...] = acc[pl.ds(first, count)].astype(BF16)


def collect_kernel(
    n_rows, n_feat, terms_ref, act_ref, gw_ref, gf_ref, out_ref, gw_out,
    mate_in, sums, chip_in, act_in, gw_in, gw_sum, gw_mate, gw_chip, gw_full,
    t_send, t_recv, c_send, c_recv, h_send, h_recv, a_send, a_recv, g_send, g_recv, e_send, e_recv,
):
    me_r, me_f = lax.axis_index("rows"), lax.axis_index("feat")
    blocks = terms_ref.shape[0] // n_rows
    edge = terms_ref.shape[2]
    quarter = blocks // n_feat
    n_chip = n_rows // 2
    chip, core = me_r // 2, me_r % 2
    mate = me_r + 1 - 2 * core
    chips = [flip(chip, p, n_chip) for p in range(n_chip)]
    peers_f = [(me_f + j) % n_feat for j in range(n_feat)]
    greet([mate] + [chips[p] * 2 + core for p in range(1, n_chip)], peers_f[1:])

    order = list(range(n_chip - 1, -1, -1))
    to_mate = {}
    for p in order:
        owner = chips[p] * 2 + 1 - core
        to_mate[p] = remote(terms_ref.at[pl.ds(owner * blocks, blocks)], mate_in.at[p],
                            t_send.at[p], t_recv.at[p], rows=mate)
        to_mate[p].start()
    gw_feat = []
    for j in range(1, n_feat):
        copy = remote(gw_ref.at[peers_f[j]], gw_in.at[me_f], g_send.at[j], g_recv.at[j], feat=peers_f[j])
        copy.start()
        gw_feat.append(copy)
    act_out = []
    for j in range(1, n_feat):
        copy = remote(act_ref.at[peers_f[j]], act_in.at[me_f], a_send.at[j], a_recv.at[j], feat=peers_f[j])
        copy.start()
        act_out.append(copy)
    act_in[me_f] = act_ref[me_f]
    gw_in[me_f] = gw_ref[me_f]
    to_chip = {}
    for p in order:
        to_mate[p].wait_recv()
        if p:
            owner = chips[p] * 2 + core

            @pl.loop(0, blocks)
            def _(i):
                sums[p, i] = (terms_ref[owner * blocks + i].astype(F32) + mate_in[p, i].astype(F32)).astype(BF16)

            to_chip[p] = remote(sums.at[p], chip_in.at[p], c_send.at[p], c_recv.at[p], rows=owner)
            to_chip[p].start()
    half = gw_in.shape[1] // 2
    for copy in gw_feat:
        copy.wait()
    gw_sum[...] = sum(gw_in[f] for f in range(n_feat))
    mine, other = pl.ds(core * half, half), pl.ds((1 - core) * half, half)
    swap = remote(gw_sum.at[other], gw_mate, e_send.at[0], e_recv.at[0], rows=mate)
    swap.start()
    swap.wait()
    gw_chip[chip] = gw_sum[mine] + gw_mate[...]
    gw_chips = []
    for p in range(1, n_chip):
        copy = remote(gw_chip.at[chip], gw_chip.at[chip], h_send.at[p], h_recv.at[p], rows=chips[p] * 2 + core)
        copy.start()
        gw_chips.append(copy)
    for copy in act_out:
        copy.wait()
    for i in range(blocks):
        out_ref[:, i * edge:(i + 1) * edge] = act_in[i // quarter, i % quarter]
    for p in range(1, n_chip):
        gw_chips[p - 1].wait_send()
        remote(gw_chip.at[chips[p]], gw_chip.at[chips[p]], h_send.at[p], h_recv.at[p], rows=mate).wait_recv()
    total_half = gw_chip[0]
    for c in range(1, n_chip):
        total_half = total_half + gw_chip[c]
    gw_full[mine] = total_half
    back = remote(gw_full.at[mine], gw_full.at[mine], e_send.at[1], e_recv.at[1], rows=mate)
    back.start()
    for p in range(1, n_chip):
        to_chip[p].wait_recv()
    for i in range(blocks):
        total = terms_ref[me_r * blocks + i].astype(F32) + mate_in[0, i].astype(F32)
        for p in range(1, n_chip):
            total = total + chip_in[p, i].astype(F32)
        gf_ref[:, i * edge:(i + 1) * edge] = total
    for p in order:
        to_mate[p].wait_send()
        if p:
            to_chip[p].wait_send()
    back.wait_send()
    remote(gw_full.at[other], gw_full.at[other], e_send.at[1], e_recv.at[1], rows=mate).wait_recv()
    gw_out[...] = gw_full[...]


def on_device(node_feats, tile_vals, tile_cols, weight, bias_vec, grad_out):
    n_rows, n_feat = lax.axis_size("rows"), lax.axis_size("feat")
    feat_loc = node_feats.shape[0]
    blocks, slots, edge = tile_vals.shape[0], tile_vals.shape[1], tile_vals.shape[2]
    feat = feat_loc * n_feat
    quarter = blocks // n_feat
    n_chip = n_rows // 2
    vmem = pl.BlockSpec(memory_space=pltpu.VMEM)
    dma = pltpu.SemaphoreType.DMA
    flops = 2 * feat_loc * blocks * slots * edge * edge
    tile_bytes = 2 * blocks * slots * edge * edge

    parts = (n_feat, quarter, feat_loc, edge)
    cols = tile_cols.T
    wide = feat + edge
    pairs = quarter // 2 if quarter % 2 == 0 else quarter
    bm, act, gw = pl.pallas_call(
        functools.partial(forward_kernel, n_rows, n_feat),
        out_shape=(
            jax.ShapeDtypeStruct(parts, BF16),
            jax.ShapeDtypeStruct(parts, BF16),
            jax.ShapeDtypeStruct((n_feat, feat_loc, wide), F32),
        ),
        in_specs=[pl.BlockSpec(memory_space=pltpu.SMEM), vmem, vmem, vmem, vmem,
                  pl.BlockSpec(memory_space=pl.ANY)],
        out_specs=(vmem,) * 3,
        scratch_shapes=[
            pltpu.VMEM((n_rows * blocks, feat_loc, edge), BF16),
            pltpu.VMEM(parts, BF16),
            pltpu.VMEM(parts, BF16),
            pltpu.VMEM((n_feat, feat_loc, feat), BF16),
            pltpu.VMEM((n_feat, feat_loc, edge), F32),
            pltpu.VMEM((blocks, slots, edge, edge), BF16),
            pltpu.VMEM(parts, BF16),
            pltpu.VMEM(parts, BF16),
            pltpu.VMEM(parts, BF16),
            dma((blocks,)),
        ] + [dma((n_chip,))] * 4 + [dma((n_feat,))] * 8 + [dma((n_feat, pairs))] * 2,
        compiler_params=pltpu.CompilerParams(
            collective_id=0, has_side_effects=True, vmem_limit_bytes=VMEM_BYTES),
        cost_estimate=pl.CostEstimate(flops=flops, bytes_accessed=tile_bytes, transcendentals=0),
        name="aggregate_and_mix",
    )(cols, node_feats, grad_out, weight.T,
      jnp.broadcast_to(bias_vec[:, None], (feat_loc, edge)), tile_vals)

    group = 4 if blocks % 4 == 0 else 1
    steps = blocks // group
    owners = 4 if n_rows % 4 == 0 else 1
    terms = pl.pallas_call(
        functools.partial(spread_kernel, blocks, slots, edge, group),
        out_shape=jax.ShapeDtypeStruct((n_rows * blocks, feat_loc, edge), BF16),
        grid_spec=pltpu.PrefetchScalarGridSpec(
            num_scalar_prefetch=1,
            grid=(steps + n_rows // owners,),
            in_specs=[
                pl.BlockSpec((blocks, feat_loc, edge), lambda i, cols: (0, 0, 0)),
                pl.BlockSpec((group, slots, edge, edge), lambda i, cols: (jnp.minimum(i, steps - 1), 0, 0, 0)),
            ],
            out_specs=pl.BlockSpec((owners * blocks, feat_loc, edge), lambda i, cols: (jnp.maximum(i - steps, 0), 0, 0)),
            scratch_shapes=[pltpu.VMEM((n_rows * blocks, feat_loc, edge), F32)],
        ),
        compiler_params=pltpu.CompilerParams(vmem_limit_bytes=VMEM_BYTES),
        cost_estimate=pl.CostEstimate(flops=flops, bytes_accessed=tile_bytes, transcendentals=0),
        name="spread_terms",
    )(cols, bm.reshape(blocks, feat_loc, edge), tile_vals)

    grad_feats, activated, gw = pl.pallas_call(
        functools.partial(collect_kernel, n_rows, n_feat),
        out_shape=(
            jax.ShapeDtypeStruct((feat_loc, blocks * edge), F32),
            jax.ShapeDtypeStruct((feat_loc, blocks * edge), BF16),
            jax.ShapeDtypeStruct((feat_loc, wide), F32),
        ),
        in_specs=[vmem] * 3,
        out_specs=(vmem,) * 3,
        scratch_shapes=[pltpu.VMEM((n_chip, blocks, feat_loc, edge), BF16)] * 3
        + [
            pltpu.VMEM(parts, BF16),
            pltpu.VMEM((n_feat, feat_loc, wide), F32),
            pltpu.VMEM((feat_loc, wide), F32),
            pltpu.VMEM((feat_loc // 2, wide), F32),
            pltpu.VMEM((n_chip, feat_loc // 2, wide), F32),
            pltpu.VMEM((feat_loc, wide), F32),
        ]
        + [dma((n_chip,))] * 6 + [dma((n_feat,))] * 4 + [dma((2,))] * 2,
        compiler_params=pltpu.CompilerParams(
            collective_id=1, has_side_effects=True, vmem_limit_bytes=VMEM_BYTES),
        cost_estimate=pl.CostEstimate(flops=1, bytes_accessed=tile_bytes // 4, transcendentals=0),
        name="collect_terms",
    )(terms, act, gw)
    grad_weight, grad_bias = gw[:, :feat].T, jnp.sum(gw[:, feat:], axis=1)
    return activated, grad_feats, grad_weight, grad_bias


def solution(mesh):
    placed = (
        P("feat", "rows"),
        P("rows", None, None, None),
        P("rows", None),
        P(None, "feat"),
        P("feat"),
        P("feat", "rows"),
    )
    return jax.shard_map(
        on_device,
        mesh=mesh,
        in_specs=placed,
        out_specs=(P("feat", "rows"), P("feat", "rows"), P(None, "feat"), P("feat")),
        check_vma=False,
    )
```

```python
import functools

import jax
import jax.numpy as jnp
from jax import lax
from jax.experimental import pallas as pl
from jax.experimental.pallas import tpu as pltpu
from jax.sharding import PartitionSpec as P

MESH = pl.DeviceIdType.MESH
BF16 = jnp.bfloat16
F32 = jnp.float32
VMEM_BYTES = 60 * 1024 * 1024


def flip(index, mask, count):
    out, place = 0, 1
    while place < count:
        bit = (index // place) % 2
        out = out + ((1 - bit) if mask & place else bit) * place
        place *= 2
    return out


def greet(rows_peers, feat_peers):
    barrier = pltpu.get_barrier_semaphore()
    for peer in rows_peers:
        pl.semaphore_signal(barrier, inc=1, device_id={"rows": peer}, device_id_type=MESH)
    for peer in feat_peers:
        pl.semaphore_signal(barrier, inc=1, device_id={"feat": peer}, device_id_type=MESH)
    pl.semaphore_wait(barrier, len(rows_peers) + len(feat_peers))


def remote(src, dst, send_sem, recv_sem, **where):
    return pltpu.make_async_remote_copy(
        src_ref=src, dst_ref=dst, send_sem=send_sem, recv_sem=recv_sem,
        device_id=where, device_id_type=MESH,
    )


def forward_kernel(
    n_rows, n_feat,
    cols_ref, x_ref, gout_ref, wt_ref, bias_ref, tiles_hbm,
    bm_in, act_out, gw_ref,
    xall, gsend, gall, wall, ball, tiles, agg_send, agg_in, bm_send,
    tile_sem, x_send, x_recv, f_send, f_recv, g_send, g_recv, w_send, w_recv,
    b_send, b_recv, a_send, a_recv, m_send, m_recv,
):
    me_r, me_f = lax.axis_index("rows"), lax.axis_index("feat")
    feat_loc = x_ref.shape[0]
    blocks, slots, edge = tiles_hbm.shape[0], tiles_hbm.shape[1], tiles_hbm.shape[2]
    quarter = blocks // n_feat
    n_chip = n_rows // 2
    chip, core = me_r // 2, me_r % 2
    mate = me_r + 1 - 2 * core
    chips = [flip(chip, p, n_chip) for p in range(n_chip)]
    peers_f = [(me_f + j) % n_feat for j in range(n_feat)]
    from_f = [(me_f + n_feat - j) % n_feat for j in range(n_feat)]

    @pl.loop(0, blocks)
    def _(i):
        pltpu.make_async_copy(tiles_hbm.at[i], tiles.at[i], tile_sem.at[i]).start()

    for i in range(blocks):
        xall[me_r * blocks + i] = x_ref[:, i * edge:(i + 1) * edge]
        gsend[i // quarter, i % quarter] = gout_ref[:, i * edge:(i + 1) * edge]

    greet([mate] + [chips[p] * 2 + core for p in range(1, n_chip)], peers_f[1:])

    half = blocks // 2
    relayed = n_chip == 4

    def owned(row, h):
        return xall.at[pl.ds(row * blocks + h * half, half)]

    def hand(origin, p, h, target):
        return remote(owned(origin, h), owned(origin, h), x_send.at[p, h], x_recv.at[p, h], rows=target)

    near = [chips[p] * 2 + core for p in range(n_chip)]
    if relayed:
        first = [(1, 0), (2, 1), (1, 1), (2, 0)]
        arrivals = first + [(3, 0), (3, 1)]
    else:
        first = arrivals = [(p, h) for p in range(1, n_chip) for h in (0, 1)]
    x_out = [hand(me_r, p, h, near[p]) for p, h in first] + [hand(me_r, 0, h, mate) for h in (0, 1)]
    for copy in x_out:
        copy.start()
    z_out = []
    for j in range(1, n_feat):
        z_out.append(remote(gsend.at[peers_f[j]], gall.at[me_f], g_send.at[j], g_recv.at[j], feat=peers_f[j]))
        z_out.append(remote(wt_ref, wall.at[me_f], w_send.at[j], w_recv.at[j], feat=peers_f[j]))
        z_out.append(remote(bias_ref, ball.at[me_f], b_send.at[j], b_recv.at[j], feat=peers_f[j]))
    for copy in z_out:
        copy.start()
    gall[me_f] = gsend[me_f]
    wall[me_f] = wt_ref[...]
    ball[me_f] = bias_ref[...]

    for p, h in arrivals:
        src = near[p]
        hand(src, p, h, mate).wait_recv()
        if relayed and (p, h) in ((1, 0), (2, 1)):
            onward = hand(src, 3, h, near[3 - p])
            onward.start()
            x_out.append(onward)
        passed = remote(owned(src, h), owned(src, h), f_send.at[p, h], f_recv.at[p, h], rows=mate)
        passed.start()
        x_out.append(passed)
    for h in (0, 1):
        hand(mate, 0, h, mate).wait_recv()
    for p, h in arrivals:
        src = chips[p] * 2 + 1 - core
        remote(owned(src, h), owned(src, h), f_send.at[p, h], f_recv.at[p, h], rows=mate).wait_recv()

    group = 4 if quarter % 4 == 0 else 1
    agg_out = []
    for j in range(1, n_feat + 1):
        q = peers_f[j % n_feat]

        @pl.loop(0, quarter // group)
        def _(g):
            first = q * quarter + g * group
            for u in range(group):
                pltpu.make_async_copy(tiles_hbm.at[first + u], tiles.at[first + u], tile_sem.at[first + u]).wait()
            for u in range(group):
                i = first + u
                picked = jnp.concatenate([xall[cols_ref[s, i]] for s in range(slots)], axis=1)
                vals = jnp.concatenate([tiles[i, s] for s in range(slots)], axis=1)
                agg = lax.dot_general(picked, vals, (((1,), (1,)), ((), ())), preferred_element_type=F32)
                agg_send[q, g * group + u] = agg.astype(BF16)

        if j < n_feat:
            copy = remote(agg_send.at[q], agg_in.at[me_f], a_send.at[j], a_recv.at[j], feat=q)
            copy.start()
            agg_out.append(copy)
    agg_in[me_f] = agg_send[me_f]

    for copy in z_out:
        copy.wait()
    for copy in agg_out:
        copy.wait()

    feat = n_feat * feat_loc
    gw_ref[...] = jnp.zeros_like(gw_ref)
    pair = 2 if quarter % 2 == 0 else 1

    def mix_copy(j, t):
        part = pl.ds(t * pair, pair)
        return remote(bm_send.at[peers_f[j], part], bm_in.at[me_f, part],
                      m_send.at[j, t], m_recv.at[j, t], feat=peers_f[j])

    @pl.loop(0, quarter // pair)
    def _(t):
        def joined(ref):
            return jnp.concatenate([ref[:, t * pair + u].reshape(feat, edge) for u in range(pair)], axis=1)

        wt = wall[...].reshape(feat, feat)
        agg = joined(agg_in)
        preact = jnp.dot(wt, agg, preferred_element_type=F32)
        preact = preact + jnp.concatenate([ball[...].reshape(feat, edge)] * pair, axis=1)
        sigma = jax.nn.sigmoid(preact)
        act = (preact * sigma).astype(BF16)
        grad = (joined(gall).astype(F32) * sigma * (1.0 + preact * (1.0 - sigma))).astype(BF16)
        mix = lax.dot_general(wt, grad, (((0,), (0,)), ((), ())), preferred_element_type=F32).astype(BF16)
        part = lax.dot_general(grad, agg, (((1,), (1,)), ((), ())), preferred_element_type=F32)
        gw_ref[:, :, :feat] += part.reshape(n_feat, feat_loc, feat)
        grad32 = grad.astype(F32)
        for u in range(pair):
            cut = slice(u * edge, (u + 1) * edge)
            act_out[:, t * pair + u] = act[:, cut].reshape(n_feat, feat_loc, edge)
            bm_send[:, t * pair + u] = mix[:, cut].reshape(n_feat, feat_loc, edge)
            gw_ref[:, :, feat:] += grad32[:, cut].reshape(n_feat, feat_loc, edge)
        for j in range(1, n_feat):
            mix_copy(j, t).start()

    bm_in[me_f] = bm_send[me_f]
    for copy in x_out:
        copy.wait_send()
    @pl.loop(0, quarter // pair)
    def _(t):
        for j in range(1, n_feat):
            mix_copy(j, t).wait()


def spread_kernel(blocks, slots, edge, group, cols_ref, bm_ref, tiles_ref, terms_ref, acc):
    step = pl.program_id(0)
    steps = blocks // group

    @pl.when(step == 0)
    def _():
        acc[...] = jnp.zeros_like(acc)

    @pl.when(step < steps)
    def _():
        for u in range(group):
            i = step * group + u
            vals = jnp.concatenate([tiles_ref[u, s] for s in range(slots)], axis=1)
            contrib = jnp.dot(bm_ref[i], vals, preferred_element_type=F32)
            for s in range(slots):
                col = cols_ref[s, i]
                acc[col] = acc[col] + contrib[:, s * edge:(s + 1) * edge]

    @pl.when(step >= steps)
    def _():
        count = terms_ref.shape[0]
        first = (step - steps) * count
        terms_ref[...] = acc[pl.ds(first, count)].astype(BF16)


def collect_kernel(
    n_rows, n_feat, terms_ref, act_ref, gw_ref, gf_ref, out_ref, gw_out, gb_out,
    mate_in, sums, chip_in, diag_in, act_in, gw_in, gw_sum, gw_mate, gw_chip, gw_full,
    t_send, t_recv, c_send, c_recv, h_send, h_recv, a_send, a_recv, g_send, g_recv, e_send, e_recv,
):
    me_r, me_f = lax.axis_index("rows"), lax.axis_index("feat")
    blocks = terms_ref.shape[0] // n_rows
    edge = terms_ref.shape[2]
    quarter = blocks // n_feat
    n_chip = n_rows // 2
    chip, core = me_r // 2, me_r % 2
    mate = me_r + 1 - 2 * core
    chips = [flip(chip, p, n_chip) for p in range(n_chip)]
    peers_f = [(me_f + j) % n_feat for j in range(n_feat)]
    greet([mate] + [chips[p] * 2 + core for p in range(1, n_chip)], peers_f[1:])

    relayed = n_chip == 4
    order = [3, 1, 2, 0] if relayed else list(range(n_chip - 1, -1, -1))
    to_mate = {}
    for p in order:
        owner = chips[p] * 2 + 1 - core
        to_mate[p] = remote(terms_ref.at[pl.ds(owner * blocks, blocks)], mate_in.at[p],
                            t_send.at[p], t_recv.at[p], rows=mate)
        to_mate[p].start()
    gw_feat = []
    for j in range(1, n_feat):
        copy = remote(gw_ref.at[peers_f[j]], gw_in.at[me_f], g_send.at[j], g_recv.at[j], feat=peers_f[j])
        copy.start()
        gw_feat.append(copy)
    act_out = []
    for j in range(1, n_feat):
        copy = remote(act_ref.at[peers_f[j]], act_in.at[me_f], a_send.at[j], a_recv.at[j], feat=peers_f[j])
        copy.start()
        act_out.append(copy)
    act_in[me_f] = act_ref[me_f]
    gw_in[me_f] = gw_ref[me_f]
    span = blocks // 2
    near = [chips[p] * 2 + core for p in range(n_chip)]
    sent = []

    def summed(p, h, extra=None):
        @pl.loop(0, span)
        def _(i):
            at = h * span + i
            total = terms_ref[near[p] * blocks + at].astype(F32) + mate_in[p, at].astype(F32)
            if extra is not None:
                total = total + extra[i].astype(F32)
            sums[p, at] = total.astype(BF16)

    def ship(p, h, target, landing, slot):
        copy = remote(sums.at[p, pl.ds(h * span, span)], landing, c_send.at[p, h], c_recv.at[slot, h], rows=near[target])
        copy.start()
        sent.append(copy)

    def landed(slot, h, landing):
        remote(landing, landing, c_send.at[slot, h], c_recv.at[slot, h], rows=mate).wait_recv()

    def chip_half(p, h):
        return chip_in.at[p, pl.ds(h * span, span)]

    if relayed:
        to_mate[3].wait_recv()
        for h in (0, 1):
            summed(3, h)
            ship(3, h, 1 + h, diag_in.at[h], 3)
        for h in (0, 1):
            to_mate[1 + h].wait_recv()
            summed(1 + h, h)
            ship(1 + h, h, 1 + h, chip_half(1 + h, h), 1 + h)
        for h in (0, 1):
            landed(3, h, diag_in.at[h])
            summed(2 - h, h, diag_in.at[h])
            ship(2 - h, h, 2 - h, chip_half(2 - h, h), 2 - h)
        to_mate[0].wait_recv()
    else:
        for p in order:
            to_mate[p].wait_recv()
            if p:
                for h in (0, 1):
                    summed(p, h)
                    ship(p, h, p, chip_half(p, h), p)
    sources = (1, 2) if relayed else tuple(range(1, n_chip))
    half = gw_in.shape[1] // 2
    for copy in gw_feat:
        copy.wait()
    gw_sum[...] = sum(gw_in[f] for f in range(n_feat))
    mine, other = pl.ds(core * half, half), pl.ds((1 - core) * half, half)
    swap = remote(gw_sum.at[other], gw_mate, e_send.at[0], e_recv.at[0], rows=mate)
    swap.start()
    swap.wait()
    gw_chip[chip] = gw_sum[mine] + gw_mate[...]
    gw_chips = []
    for p in range(1, n_chip):
        copy = remote(gw_chip.at[chip], gw_chip.at[chip], h_send.at[p], h_recv.at[p], rows=chips[p] * 2 + core)
        copy.start()
        gw_chips.append(copy)
    for copy in act_out:
        copy.wait()
    for i in range(blocks):
        out_ref[:, i * edge:(i + 1) * edge] = act_in[i // quarter, i % quarter]
    for p in range(1, n_chip):
        gw_chips[p - 1].wait_send()
        remote(gw_chip.at[chips[p]], gw_chip.at[chips[p]], h_send.at[p], h_recv.at[p], rows=mate).wait_recv()
    total_half = gw_chip[0]
    for c in range(1, n_chip):
        total_half = total_half + gw_chip[c]
    gw_full[mine] = total_half
    back = remote(gw_full.at[mine], gw_full.at[mine], e_send.at[1], e_recv.at[1], rows=mate)
    back.start()
    for p in sources:
        for h in (0, 1):
            landed(p, h, chip_half(p, h))
    for i in range(blocks):
        total = terms_ref[me_r * blocks + i].astype(F32) + mate_in[0, i].astype(F32)
        for p in sources:
            total = total + chip_in[p, i].astype(F32)
        gf_ref[:, i * edge:(i + 1) * edge] = total
    for p in order:
        to_mate[p].wait_send()
    for copy in sent:
        copy.wait_send()
    back.wait_send()
    remote(gw_full.at[other], gw_full.at[other], e_send.at[1], e_recv.at[1], rows=mate).wait_recv()
    gw_out[...] = gw_full[:, :gw_out.shape[1]]
    gb_out[...] = gw_full[:, gw_out.shape[1]:]


def on_device(node_feats, tile_vals, tile_cols, weight, bias_vec, grad_out):
    n_rows, n_feat = lax.axis_size("rows"), lax.axis_size("feat")
    feat_loc = node_feats.shape[0]
    blocks, slots, edge = tile_vals.shape[0], tile_vals.shape[1], tile_vals.shape[2]
    feat = feat_loc * n_feat
    quarter = blocks // n_feat
    n_chip = n_rows // 2
    vmem = pl.BlockSpec(memory_space=pltpu.VMEM)
    dma = pltpu.SemaphoreType.DMA
    flops = 2 * feat_loc * blocks * slots * edge * edge
    tile_bytes = 2 * blocks * slots * edge * edge

    parts = (n_feat, quarter, feat_loc, edge)
    cols = tile_cols.T
    wide = feat + edge
    pairs = quarter // 2 if quarter % 2 == 0 else quarter
    bm, act, gw = pl.pallas_call(
        functools.partial(forward_kernel, n_rows, n_feat),
        out_shape=(
            jax.ShapeDtypeStruct(parts, BF16),
            jax.ShapeDtypeStruct(parts, BF16),
            jax.ShapeDtypeStruct((n_feat, feat_loc, wide), F32),
        ),
        in_specs=[pl.BlockSpec(memory_space=pltpu.SMEM), vmem, vmem, vmem, vmem,
                  pl.BlockSpec(memory_space=pl.ANY)],
        out_specs=(vmem,) * 3,
        scratch_shapes=[
            pltpu.VMEM((n_rows * blocks, feat_loc, edge), BF16),
            pltpu.VMEM(parts, BF16),
            pltpu.VMEM(parts, BF16),
            pltpu.VMEM((n_feat, feat_loc, feat), BF16),
            pltpu.VMEM((n_feat, feat_loc, edge), F32),
            pltpu.VMEM((blocks, slots, edge, edge), BF16),
            pltpu.VMEM(parts, BF16),
            pltpu.VMEM(parts, BF16),
            pltpu.VMEM(parts, BF16),
            dma((blocks,)),
        ] + [dma((n_chip, 2))] * 4 + [dma((n_feat,))] * 8 + [dma((n_feat, pairs))] * 2,
        compiler_params=pltpu.CompilerParams(
            collective_id=0, has_side_effects=True, vmem_limit_bytes=VMEM_BYTES),
        cost_estimate=pl.CostEstimate(flops=flops, bytes_accessed=tile_bytes, transcendentals=0),
        name="aggregate_and_mix",
    )(cols, node_feats, grad_out, weight.T,
      jnp.broadcast_to(bias_vec[:, None], (feat_loc, edge)), tile_vals)

    group = 4 if blocks % 4 == 0 else 1
    steps = blocks // group
    owners = 4 if n_rows % 4 == 0 else 1
    terms = pl.pallas_call(
        functools.partial(spread_kernel, blocks, slots, edge, group),
        out_shape=jax.ShapeDtypeStruct((n_rows * blocks, feat_loc, edge), BF16),
        grid_spec=pltpu.PrefetchScalarGridSpec(
            num_scalar_prefetch=1,
            grid=(steps + n_rows // owners,),
            in_specs=[
                pl.BlockSpec((blocks, feat_loc, edge), lambda i, cols: (0, 0, 0)),
                pl.BlockSpec((group, slots, edge, edge), lambda i, cols: (jnp.minimum(i, steps - 1), 0, 0, 0)),
            ],
            out_specs=pl.BlockSpec((owners * blocks, feat_loc, edge), lambda i, cols: (jnp.maximum(i - steps, 0), 0, 0)),
            scratch_shapes=[pltpu.VMEM((n_rows * blocks, feat_loc, edge), F32)],
        ),
        compiler_params=pltpu.CompilerParams(vmem_limit_bytes=VMEM_BYTES),
        cost_estimate=pl.CostEstimate(flops=flops, bytes_accessed=tile_bytes, transcendentals=0),
        name="spread_terms",
    )(cols, bm.reshape(blocks, feat_loc, edge), tile_vals)

    grad_feats, activated, gw, gb = pl.pallas_call(
        functools.partial(collect_kernel, n_rows, n_feat),
        out_shape=(
            jax.ShapeDtypeStruct((feat_loc, blocks * edge), F32),
            jax.ShapeDtypeStruct((feat_loc, blocks * edge), BF16),
            jax.ShapeDtypeStruct((feat_loc, feat), F32),
            jax.ShapeDtypeStruct((feat_loc, edge), F32),
        ),
        in_specs=[vmem] * 3,
        out_specs=(vmem,) * 4,
        scratch_shapes=[pltpu.VMEM((n_chip, blocks, feat_loc, edge), BF16)] * 3
        + [
            pltpu.VMEM((2, blocks // 2, feat_loc, edge), BF16),
            pltpu.VMEM(parts, BF16),
            pltpu.VMEM((n_feat, feat_loc, wide), F32),
            pltpu.VMEM((feat_loc, wide), F32),
            pltpu.VMEM((feat_loc // 2, wide), F32),
            pltpu.VMEM((n_chip, feat_loc // 2, wide), F32),
            pltpu.VMEM((feat_loc, wide), F32),
        ]
        + [dma((n_chip,))] * 2 + [dma((n_chip, 2))] * 2 + [dma((n_chip,))] * 2 + [dma((n_feat,))] * 4 + [dma((2,))] * 2,
        compiler_params=pltpu.CompilerParams(
            collective_id=1, has_side_effects=True, vmem_limit_bytes=VMEM_BYTES),
        cost_estimate=pl.CostEstimate(flops=1, bytes_accessed=tile_bytes // 4, transcendentals=0),
        name="collect_terms",
    )(terms, act, gw)
    grad_weight, grad_bias = gw.T, jnp.sum(gb, axis=1)
    return activated, grad_feats, grad_weight, grad_bias


def solution(mesh):
    placed = (
        P("feat", "rows"),
        P("rows", None, None, None),
        P("rows", None),
        P(None, "feat"),
        P("feat"),
        P("feat", "rows"),
    )
    return jax.shard_map(
        on_device,
        mesh=mesh,
        in_specs=placed,
        out_specs=(P("feat", "rows"), P("feat", "rows"), P(None, "feat"), P("feat")),
        check_vma=False,
    )
```
